32 devices in a mesh: runs: 2 (over y), space: 4 (over z), sub: 2 (over x), lane: 2 (over core).
Axes of the slice: x: 2, y: 2, z: 4, core: 2. Of those that a mesh axis runs over, the one named last changes fastest.
Arguments:
- fine_moments: bfloat16 [81, 6144], P(None, ('runs', 'space', 'sub', 'lane')), parts along dimension 1, may hold values from -6 to 6
- coarse_moments: bfloat16 [81, 512], P(None, ('runs', 'space', 'sub', 'lane')), parts along dimension 1, may hold values from -12 to 12
- m2l_table: bfloat16 [158, 81, 81], replicated, may hold values from -0.078125 to 0.078125
- fine_pairs: int32 [3, 196608], P(None, ('runs', 'space', 'sub', 'lane')), parts along dimension 1, may hold values from 0 to 3071, as said below
- coarse_pairs: int32 [3, 65536], P(None, ('runs', 'space', 'sub', 'lane')), parts along dimension 1, may hold values from 0 to 255, as said below
Outputs:
- fine_local: float32 [81, 6144], P(None, ('runs', 'space', 'sub', 'lane')), parts along dimension 1
- coarse_local: float32 [81, 512], P(None, ('runs', 'space', 'sub', 'lane')), parts along dimension 1
The draws below stay inside these ranges and needn't reach their ends.
There are 2 independent parts, one for each index of `runs`. The reference program is written for one: setup_inputs(seed, part) draws one part's arguments, and reference() takes and returns one part's arrays. A program takes and returns all parts, laid end to end along the dimension named above; an argument that names none is the same for every part. Nothing has to cross between parts.
Inputs may be any that keep to these rules, and one draw needn't show every extreme that they name: `fine_pairs`: row 0 holds source cells, row 1 target cells, row 2 offset classes. The 6144 slots of one device come in aligned blocks of 128 with one class each; class 158 marks an empty block, whose pairs add nothing. A device's target cells lie in its own group of 768 consecutive cells (the group of its index along space), its source cells in that group or one of the two beside it. `coarse_pairs`: row 0 holds source cells, row 1 target cells, row 2 offset classes. The 2048 slots of one device come in aligned blocks of 128 with one class each; class 158 marks an empty block. A device's target cells are among its own 16 cells; its source cells lie in its own group of 64 consecutive coarse cells (the group of its index along space) or one of the two beside it.
All inputs are finite; a program needn't handle non-finite values.
Results may differ from the reference program's by a relative error of at most 0.0003.
Values may be sent and summed in bfloat16 or wider, within the bound.
A program may use at most 64 MiB of HBM per device.

```python
import jax
import jax.numpy as jnp
from jax import lax

K = 81
OFFS = 158
BLK = 128
CF_DEV = 192
CC_DEV = 16
FP_DEV = 6144
CP_DEV = 2048
GROUP = 768
CGROUP = 64
NF = 3072
NC = 256
N_SPACE = 4
N_SUB = 2
N_LANE = 2


def live_classes(key, devices, nblocks):
    keys = jax.random.split(key, 3)
    live = jax.random.randint(keys[0], (devices,), nblocks // 2, nblocks + 1)
    fuller = jax.random.randint(keys[1], (), 1, devices)
    live = jnp.where(jnp.arange(devices) == fuller, nblocks, live)
    live = live.at[0].set(nblocks // 2)
    classes = jax.random.randint(keys[2], (devices, nblocks), 0, OFFS)
    classes = jnp.where(jnp.arange(nblocks)[None, :] < live[:, None], classes, OFFS)
    return jnp.repeat(classes, BLK, axis=1)


def draw_fine_pairs(key, part):
    key = jax.random.fold_in(key, 11)
    keys = jax.random.split(key, 4)
    devices = N_SPACE * N_SUB * N_LANE
    members = N_SUB * N_LANE
    owner = jnp.arange(devices)[:, None] // members
    target = owner * GROUP + jax.random.randint(keys[0], (devices, FP_DEV), 0, GROUP)
    side = jnp.clip(owner + jax.random.randint(keys[1], (devices, FP_DEV), -1, 2), 0, N_SPACE - 1)
    source = side * GROUP + jax.random.randint(keys[2], (devices, FP_DEV), 0, GROUP)
    source = source.at[0, 0].set(0)
    target = target.at[devices - 1, 0].set(NF - 1)
    classes = live_classes(keys[3], devices, FP_DEV // BLK)
    return jnp.stack([source, target, classes]).reshape(3, devices * FP_DEV).astype(jnp.int32)


def draw_coarse_pairs(key, part):
    key = jax.random.fold_in(key, 23)
    keys = jax.random.split(key, 4)
    devices = N_SPACE * N_SUB * N_LANE
    members = N_SUB * N_LANE
    device = jnp.arange(devices)[:, None]
    owner = device // members
    target = device * CC_DEV + jax.random.randint(keys[0], (devices, CP_DEV), 0, CC_DEV)
    side = jnp.clip(owner + jax.random.randint(keys[1], (devices, CP_DEV), -1, 2), 0, N_SPACE - 1)
    source = side * CGROUP + jax.random.randint(keys[2], (devices, CP_DEV), 0, CGROUP)
    source = source.at[0, 0].set(0)
    target = target.at[devices - 1, 0].set(NC - 1)
    classes = live_classes(keys[3], devices, CP_DEV // BLK)
    return jnp.stack([source, target, classes]).reshape(3, devices * CP_DEV).astype(jnp.int32)


def level_of(rng, shape, shards, low, high):
    loudness = 1.0
    for dim, shards_of in shards:
        heights = jax.random.uniform(jax.random.fold_in(jax.random.fold_in(rng, 6), dim), (shards_of,), jnp.float32, low / len(shards), high / len(shards))
        loudness = loudness * jnp.repeat(jnp.exp(heights), shape[dim] // shards_of).reshape((-1,) + (1,) * (len(shape) - 1 - dim))
    return loudness


def bell_draw(stream_key, shape, spread, bound, cuts=(), dtype=jnp.bfloat16):
    gain = level_of(stream_key, shape, cuts, -0.22, 0.18) if cuts else 1.0
    values = jax.random.normal(stream_key, shape, jnp.float32) * spread * gain
    return jnp.minimum(jnp.maximum(values, -bound), bound).astype(dtype)


def setup_inputs(seed: int = 0, part: int = 0) -> dict:
    key_list = jax.random.split(jax.random.key(seed), 6)
    part_keys = jax.random.split(jax.random.fold_in(key_list[5], part), 6)
    fine_moments = bell_draw(part_keys[0], (K, NF), 1.0, 6.0, ((1, 16),))
    coarse_moments = bell_draw(part_keys[1], (K, NC), 2.0, 12.0, ((1, 16),))
    m2l_table = bell_draw(key_list[2], (OFFS, K, K), (K * 2 * FP_DEV // CF_DEV) ** -0.5, 0.078125)
    fine_pairs = draw_fine_pairs(jax.random.fold_in(jax.random.fold_in(key_list[5], part), 71), part)
    coarse_pairs = draw_coarse_pairs(jax.random.fold_in(jax.random.fold_in(key_list[5], part), 71), part)
    return {"fine_moments": fine_moments, "coarse_moments": coarse_moments, "m2l_table": m2l_table, "fine_pairs": fine_pairs, "coarse_pairs": coarse_pairs}


def degree_sign(count):
    index = jnp.arange(count)
    squares = jnp.arange(1, 17) ** 2
    degree = jnp.sum((index[:, None] >= squares[None, :]).astype(jnp.int32), axis=1)
    return jnp.where(degree % 2 == 1, -1.0, 1.0).astype(jnp.float32)


def pair_terms(moments, piece, table, parity, total):
    source = piece[0]
    target = piece[1]
    nblocks = source.shape[0] // BLK
    src_b = source.reshape(nblocks, BLK)
    tgt_b = target.reshape(nblocks, BLK)
    fetch = jnp.stack([src_b, tgt_b], axis=1).reshape(-1)
    store = jnp.stack([tgt_b, src_b], axis=1).reshape(-1)
    flips = jnp.stack([jnp.ones_like(parity), parity], axis=1)
    picked = moments[:, fetch].reshape(K, nblocks, 2, BLK) * flips[:, None, :, None]
    operators = table[piece[2].reshape(nblocks, BLK)[:, 0]]
    result = jnp.einsum("bij,jbsn->ibsn", operators, picked)
    result = result * flips[:, None, :, None]
    return total.at[:, store].add(result.reshape(K, -1))


def accumulate(moments, pairs, table, parity, per_dev, cells):
    turns = pairs.shape[1] // per_dev
    pieces = pairs.reshape(3, turns, per_dev).transpose(1, 0, 2)

    def step(total, piece):
        return pair_terms(moments, piece, table, parity, total), None

    total, _ = lax.scan(step, jnp.zeros((K, cells), jnp.float32), pieces)
    return total


def reference(fine_moments, coarse_moments, m2l_table, fine_pairs, coarse_pairs):
    parity = degree_sign(K)
    table = jnp.concatenate([m2l_table.astype(jnp.float32), jnp.zeros((1, K, K), jnp.float32)], axis=0)
    fine_local = accumulate(fine_moments.astype(jnp.float32), fine_pairs, table, parity, FP_DEV, NF)
    coarse_local = accumulate(coarse_moments.astype(jnp.float32), coarse_pairs, table, parity, CP_DEV, NC)
    return fine_local, coarse_local
```

```python
import functools

import jax
import jax.numpy as jnp
from jax import lax
from jax.experimental import pallas as pl
from jax.experimental.pallas import tpu as pltpu
from jax.sharding import PartitionSpec as P

BLK = 128
STEP = 256
LANES = 256
ROWS = 96
F32 = jnp.float32
BF16 = jnp.bfloat16


def divider(width, limit):
    for shift in range(31):
        mul = -(-(1 << shift) // width)
        if all((w * mul) >> shift == w // width for w in range(limit)):
            break
    assert limit * mul < 2**31
    return lambda w: (w * mul) >> shift


def row_sign(rows, dtype):
    index = lax.broadcasted_iota(jnp.int32, (rows, 1), 0)
    degree = jnp.zeros((rows, 1), jnp.int32)
    for root in range(1, 17):
        degree = degree + jnp.where(index >= root * root, 1, 0)
    return (1 - 2 * (degree & 1)).astype(F32).astype(dtype)


def split(values):
    top = values.astype(BF16)
    return top, (values - top.astype(F32)).astype(BF16)


def one_hot(lo):
    index = lax.broadcasted_iota(jnp.int32, (LANES, STEP), 0)
    return jnp.where(index == lo, 1.0, 0.0).astype(BF16)


def pick(stack, first, count, hi, hot):
    height = stack.shape[1]
    block = stack[first : first + count].reshape(count * height, LANES)
    all_parts = jnp.dot(block, hot, preferred_element_type=F32)
    got = jnp.zeros((height, STEP), F32)
    for h in range(count):
        got = jnp.where(hi == first + h, all_parts[h * height : (h + 1) * height], got)
    return got


def put(acc, first, count, hi, hot, values):
    height = values.shape[0]
    top, rest = split(values)
    both = jnp.concatenate([top, rest], axis=1)
    hi2 = jnp.concatenate([hi, hi], axis=1)
    spread = jnp.concatenate(
        [
            both * jnp.where(hi2 == first + h, 1.0, 0.0).astype(BF16)
            for h in range(count)
        ],
        axis=0,
    )
    hot2 = jnp.concatenate([hot, hot], axis=1)
    total = lax.dot_general(
        spread, hot2, (((1,), (1,)), ((), ())), preferred_element_type=F32
    )
    acc[...] += total.reshape(count, height, LANES)


def level(
    pairs, classes, table, stack, flipped, acc_src, acc_tgt, res, offset, width, mid, cells
):
    width_of = divider(width, cells)
    classes_count = table.shape[0]
    k = table.shape[1]
    src_count = stack.shape[0]
    first, tgt_count = mid

    def step(i, carry):
        base = pl.multiple_of(i * STEP, STEP)
        src = pairs[0:1, pl.ds(base, STEP)] - offset
        tgt = pairs[1:2, pl.ds(base, STEP)] - offset
        live = pairs[2:3, pl.ds(base, STEP)] < classes_count
        src_hi = width_of(src)
        tgt_hi = width_of(tgt)
        src_hot = one_hot(src - src_hi * width)
        tgt_hot = one_hot(tgt - tgt_hi * width)
        src_hi = jnp.where(live, src_hi, -1)
        tgt_hi = jnp.where(live, tgt_hi, -1)
        from_src = pick(stack, 0, src_count, src_hi, src_hot)
        from_tgt = pick(flipped, first, tgt_count, tgt_hi, tgt_hot)
        for j in range(STEP // BLK):
            at = slice(j * BLK, (j + 1) * BLK)
            operand = jnp.concatenate([from_src[:, at], from_tgt[:, at]], axis=1).astype(BF16)
            kind = jnp.minimum(classes[2, base + j * BLK], classes_count - 1)
            moved = jnp.dot(table[kind], operand[:k], preferred_element_type=F32)
            res[0, :k, at] = moved[:, :BLK]
            res[1, :k, at] = moved[:, BLK:]
        put(acc_tgt, first, tgt_count, tgt_hi, tgt_hot, res[0])
        put(acc_src, 0, src_count, src_hi, src_hot, res[1])
        return carry

    lax.fori_loop(0, pairs.shape[1] // STEP, step, 0)


def compute(
    sizes,
    fine_stack,
    coarse_stack,
    table,
    fine_pairs,
    coarse_pairs,
    fine_classes,
    coarse_classes,
    fine_out,
    coarse_out,
    fine_flip,
    coarse_flip,
    fine_tgt,
    coarse_tgt,
    res,
):
    cf, cc, members, axis = sizes
    place = lax.axis_index(axis) - 1
    sign_b = row_sign(ROWS, BF16)
    sign_f = row_sign(ROWS, F32)
    fine_flip[...] = fine_stack[...] * sign_b
    coarse_flip[...] = coarse_stack[...] * sign_b
    for ref in (fine_out, coarse_out, fine_tgt, coarse_tgt, res):
        ref[...] = jnp.zeros(ref.shape, ref.dtype)
    level(
        fine_pairs, fine_classes, table, fine_stack, fine_flip, fine_out, fine_tgt, res,
        place * members * cf, cf, (members, members), 3 * members * cf,
    )
    level(
        coarse_pairs, coarse_classes, table, coarse_stack, coarse_flip, coarse_out, coarse_tgt,
        res, place * members * cc, LANES, (0, coarse_stack.shape[0]), 3 * members * cc,
    )
    fine_out[...] = fine_out[...] * sign_f
    fine_out[members : 2 * members] += fine_tgt[...]
    coarse_out[...] = coarse_out[...] * sign_f + coarse_tgt[...]


def from_behind(shard, axis, by):
    size = lax.axis_size(axis)
    pairs = [(i, i + by) for i in range(size) if 0 <= i + by < size]
    return lax.ppermute(shard, axis, pairs)


def per_device(fine_moments, coarse_moments, m2l_table, fine_pairs, coarse_pairs):
    k, cf = fine_moments.shape
    cc = coarse_moments.shape[1]
    members = lax.axis_size("sub") * lax.axis_size("lane")
    slots = 3 * members
    mine = jnp.concatenate([fine_moments, coarse_moments], axis=1)
    mine = jnp.pad(mine, ((0, ROWS - k), (0, LANES - cf - cc)))
    group = lax.all_gather(mine, ("sub", "lane"), axis=0, tiled=False)
    fine_stack = jnp.concatenate(
        [from_behind(group, "space", 1), group, from_behind(group, "space", -1)], axis=0
    )
    coarse_wide = slots * cc
    coarse_slots = -(-coarse_wide // LANES)
    coarse_stack = fine_stack[:, :, cf : cf + cc].transpose(1, 0, 2).reshape(ROWS, coarse_wide)
    coarse_stack = jnp.pad(coarse_stack, ((0, 0), (0, coarse_slots * LANES - coarse_wide)))
    coarse_stack = coarse_stack.reshape(ROWS, coarse_slots, LANES).transpose(1, 0, 2)
    vmem = pl.BlockSpec(memory_space=pltpu.VMEM)
    smem = pl.BlockSpec(memory_space=pltpu.SMEM)
    fine_part, coarse_part = pl.pallas_call(
        functools.partial(compute, (cf, cc, members, "space")),
        out_shape=(
            jax.ShapeDtypeStruct((slots, ROWS, LANES), F32),
            jax.ShapeDtypeStruct((coarse_slots, ROWS, LANES), F32),
        ),
        in_specs=[vmem] * 5 + [smem] * 2,
        out_specs=(vmem, vmem),
        scratch_shapes=[
            pltpu.VMEM((slots, ROWS, LANES), BF16),
            pltpu.VMEM((coarse_slots, ROWS, LANES), BF16),
            pltpu.VMEM((members, ROWS, LANES), F32),
            pltpu.VMEM((coarse_slots, ROWS, LANES), F32),
            pltpu.VMEM((2, ROWS, STEP), F32),
        ],
        compiler_params=pltpu.CompilerParams(vmem_limit_bytes=48 * 1024 * 1024),
    )(fine_stack, coarse_stack, m2l_table, fine_pairs, coarse_pairs, fine_pairs, coarse_pairs)
    coarse_part = coarse_part.transpose(1, 0, 2).reshape(ROWS, coarse_slots * LANES)
    coarse_part = coarse_part[:, :coarse_wide].reshape(ROWS, slots, cc).transpose(1, 0, 2)
    part = jnp.concatenate([fine_part[:, :k, :cf], coarse_part[:, :k]], axis=2)
    middle = (
        part[members : 2 * members]
        + from_behind(part[:members], "space", -1)
        + from_behind(part[2 * members :], "space", 1)
    )
    local = lax.psum_scatter(middle, ("sub", "lane"), scatter_dimension=0, tiled=False)
    return local[:, :cf], local[:, cf:]


def solution(mesh):
    cells = P(None, ("runs", "space", "sub", "lane"))
    return jax.shard_map(
        per_device,
        mesh=mesh,
        in_specs=(cells, cells, P(), cells, cells),
        out_specs=(cells, cells),
        check_vma=False,
    )
```

```python
import functools

import jax
import jax.numpy as jnp
from jax import lax
from jax.experimental import pallas as pl
from jax.experimental.pallas import tpu as pltpu
from jax.sharding import PartitionSpec as P

BLK = 128
STEP = 256
LANES = 256
ROWS = 96
F32 = jnp.float32
BF16 = jnp.bfloat16


def divider(width, limit):
    for shift in range(31):
        mul = -(-(1 << shift) // width)
        if all((w * mul) >> shift == w // width for w in range(limit)):
            break
    assert limit * mul < 2**31
    return lambda w: (w * mul) >> shift


def row_sign(rows, dtype):
    index = lax.broadcasted_iota(jnp.int32, (rows, 1), 0)
    degree = jnp.zeros((rows, 1), jnp.int32)
    for root in range(1, 17):
        degree = degree + jnp.where(index >= root * root, 1, 0)
    return (1 - 2 * (degree & 1)).astype(F32).astype(dtype)


def split(values):
    top = values.astype(BF16)
    return top, (values - top.astype(F32)).astype(BF16)


def one_hot(lo):
    index = lax.broadcasted_iota(jnp.int32, (LANES, STEP), 0)
    return jnp.where(index == lo, 1.0, 0.0).astype(BF16)


def pick(stack, hi, hot):
    count = stack.shape[0]
    height = stack.shape[1]
    block = stack[...].reshape(count * height, LANES)
    all_parts = jnp.dot(block, hot, preferred_element_type=F32)
    got = jnp.zeros((height, STEP), F32)
    for h in range(count):
        got = jnp.where(hi == h, all_parts[h * height : (h + 1) * height], got)
    return got


def put(acc, hi, hot, values):
    count = acc.shape[0]
    height = values.shape[0]
    top, rest = split(values)
    both = jnp.concatenate([top, rest], axis=1)
    hi2 = jnp.concatenate([hi, hi], axis=1)
    spread = jnp.concatenate(
        [
            both * jnp.where(hi2 == h, 1.0, 0.0).astype(BF16)
            for h in range(count)
        ],
        axis=0,
    )
    hot2 = jnp.concatenate([hot, hot], axis=1)
    total = lax.dot_general(
        spread, hot2, (((1,), (1,)), ((), ())), preferred_element_type=F32
    )
    acc[...] += total.reshape(count, height, LANES)


def level(
    pairs, classes, table, stack, flipped, acc_src, acc_tgt, res, offset, width, first, cells
):
    width_of = divider(width, cells)
    classes_count = table.shape[0]
    k = table.shape[1]

    def step(i, carry):
        base = pl.multiple_of(i * STEP, STEP)
        src = pairs[0:1, pl.ds(base, STEP)] - offset
        tgt = pairs[1:2, pl.ds(base, STEP)] - offset
        live = pairs[2:3, pl.ds(base, STEP)] < classes_count
        src_hi = width_of(src)
        tgt_hi = width_of(tgt)
        src_hot = one_hot(src - src_hi * width)
        tgt_hot = one_hot(tgt - tgt_hi * width)
        src_hi = jnp.where(live, src_hi, -1)
        tgt_hi = jnp.where(live, tgt_hi - first, -1)
        from_src = pick(stack, src_hi, src_hot)
        from_tgt = pick(flipped, tgt_hi, tgt_hot)
        for j in range(STEP // BLK):
            at = slice(j * BLK, (j + 1) * BLK)
            operand = jnp.concatenate([from_src[:, at], from_tgt[:, at]], axis=1).astype(BF16)
            kind = jnp.minimum(classes[2, base + j * BLK], classes_count - 1)
            moved = jnp.dot(table[kind], operand[:k], preferred_element_type=F32)
            res[0, :k, at] = moved[:, :BLK]
            res[1, :k, at] = moved[:, BLK:]
        put(acc_tgt, tgt_hi, tgt_hot, res[0])
        put(acc_src, src_hi, src_hot, res[1])
        return carry

    lax.fori_loop(0, pairs.shape[1] // STEP, step, 0)


def kernel(
    sizes,
    mine_hbm,
    table_hbm,
    fine_hbm,
    coarse_hbm,
    fine_out,
    coarse_out,
    window,
    fine_flip,
    coarse_stack,
    coarse_flip,
    part,
    coarse_part,
    fine_tgt,
    coarse_tgt,
    res,
    arrived,
    table,
    fine_pairs,
    coarse_pairs,
    fine_classes,
    coarse_classes,
    local_sems,
    send_in,
    recv_in,
    send_out,
    recv_out,
):
    cf, cc, subs, lanes, spaces = sizes
    members = subs * lanes
    k = fine_out.shape[0]
    rows = arrived.shape[1]
    space = lax.axis_index("space")
    me = lax.axis_index("sub") * lanes + lax.axis_index("lane")

    local = [
        pltpu.make_async_copy(source, target, local_sems.at[n])
        for n, (source, target) in enumerate(
            (
                (table_hbm, table),
                (fine_hbm, fine_pairs),
                (coarse_hbm, coarse_pairs),
                (fine_hbm, fine_classes),
                (coarse_hbm, coarse_classes),
            )
        )
    ]
    for copy in local:
        copy.start()

    def partners(act, away_first=True):
        for step in (-1, 1, 0) if away_first else (0, -1, 1):
            for member in range(members):
                there = space + step
                near = jnp.logical_and(there >= 0, there < spaces)
                if step == 0:
                    near = member != me
                target = {
                    "space": there,
                    "sub": jnp.int32(member // lanes),
                    "lane": jnp.int32(member % lanes),
                }
                theirs = (1 + step) * members + member
                ours = (1 - step) * members + me
                pl.when(near)(functools.partial(act, target, theirs, ours))

    barrier = pltpu.get_barrier_semaphore()

    def greet(target, theirs, ours):
        pl.semaphore_signal(
            barrier, inc=1, device_id=target, device_id_type=pl.DeviceIdType.MESH
        )

    partners(greet)
    window[pl.ds(members + me, 1)] = mine_hbm[...][None]
    for step in (-1, 1):
        there = space + step
        first = (1 + step) * members

        @pl.when(jnp.logical_not(jnp.logical_and(there >= 0, there < spaces)))
        def _():
            window[first : first + members] = jnp.zeros((members, ROWS, LANES), BF16)

    beside = jnp.where(space > 0, 1, 0) + jnp.where(space < spaces - 1, 1, 0)
    pl.semaphore_wait(barrier, members - 1 + members * beside)

    def give(target, theirs, ours):
        return pltpu.make_async_remote_copy(
            src_ref=mine_hbm,
            dst_ref=window.at[ours],
            send_sem=send_in.at[theirs],
            recv_sem=recv_in.at[ours],
            device_id=target,
            device_id_type=pl.DeviceIdType.MESH,
        )

    def take(target, theirs, ours):
        return pltpu.make_async_remote_copy(
            src_ref=mine_hbm,
            dst_ref=window.at[theirs],
            send_sem=send_in.at[theirs],
            recv_sem=recv_in.at[theirs],
            device_id=target,
            device_id_type=pl.DeviceIdType.MESH,
        )

    partners(lambda *at: give(*at).start())
    for ref in (part, coarse_part, fine_tgt, coarse_tgt, res):
        ref[...] = jnp.zeros(ref.shape, ref.dtype)
    coarse_stack[...] = jnp.zeros(coarse_stack.shape, BF16)
    partners(lambda *at: take(*at).wait_recv())
    partners(lambda *at: give(*at).wait_send())

    sign_b = row_sign(ROWS, BF16)
    sign_f = row_sign(ROWS, F32)
    fine_flip[...] = window[members : 2 * members] * sign_b
    for slot in range(3 * members):
        h, at = divmod(slot * cc, LANES)
        coarse_stack[h, :, at : at + cc] = window[slot, :, cf : cf + cc]
    coarse_flip[...] = coarse_stack[...] * sign_b
    for copy in local:
        copy.wait()
    place = space - 1
    level(
        coarse_pairs, coarse_classes, table, coarse_stack, coarse_flip, coarse_part, coarse_tgt,
        res, place * members * cc, LANES, 0, 3 * members * cc,
    )
    level(
        fine_pairs, fine_classes, table, window, fine_flip, part, fine_tgt, res,
        place * members * cf, cf, members, 3 * members * cf,
    )
    coarse_part[...] = coarse_part[...] * sign_f + coarse_tgt[...]
    for slot in range(3 * members):
        h, at = divmod(slot * cc, LANES)
        total = part[slot] * sign_f
        if members <= slot < 2 * members:
            total = total + fine_tgt[slot - members]
        part[slot] = total
        part[slot, :, cf : cf + cc] = coarse_part[h, :, at : at + cc]

    def hand(target, theirs, ours):
        return pltpu.make_async_remote_copy(
            src_ref=part.at[theirs, 0:rows],
            dst_ref=arrived.at[ours],
            send_sem=send_out.at[theirs],
            recv_sem=recv_out.at[ours],
            device_id=target,
            device_id_type=pl.DeviceIdType.MESH,
        )

    def catch(target, theirs, ours):
        return pltpu.make_async_remote_copy(
            src_ref=part.at[theirs, 0:rows],
            dst_ref=arrived.at[theirs],
            send_sem=send_out.at[theirs],
            recv_sem=recv_out.at[theirs],
            device_id=target,
            device_id_type=pl.DeviceIdType.MESH,
        )

    partners(lambda *at: hand(*at).start())
    res[0, :rows] = part[pl.ds(members + me, 1), 0:rows][0]

    def gather(target, theirs, ours):
        catch(target, theirs, ours).wait_recv()
        res[0, :rows] += arrived[theirs]

    partners(gather, away_first=False)
    fine_out[...] = res[0, :k, :cf]
    coarse_out[...] = res[0, :k, cf : cf + cc]
    partners(lambda *at: hand(*at).wait_send())


def per_device(spaces, fine_moments, coarse_moments, m2l_table, fine_pairs, coarse_pairs):
    k, cf = fine_moments.shape
    cc = coarse_moments.shape[1]
    subs, lanes = lax.axis_size("sub"), lax.axis_size("lane")
    members = subs * lanes
    slots = 3 * members
    rows = -(-k // 8) * 8
    coarse_slots = -(-slots * cc // LANES)
    mine = jnp.concatenate([fine_moments, coarse_moments], axis=1)
    mine = jnp.pad(mine, ((0, ROWS - k), (0, LANES - cf - cc)))
    vmem = pl.BlockSpec(memory_space=pltpu.VMEM)
    anywhere = pl.BlockSpec(memory_space=pl.ANY)
    return pl.pallas_call(
        functools.partial(kernel, (cf, cc, subs, lanes, spaces)),
        out_shape=(
            jax.ShapeDtypeStruct((k, cf), F32),
            jax.ShapeDtypeStruct((k, cc), F32),
        ),
        in_specs=[vmem, anywhere, anywhere, anywhere],
        out_specs=(vmem, vmem),
        scratch_shapes=[
            pltpu.VMEM((slots, ROWS, LANES), BF16),
            pltpu.VMEM((members, ROWS, LANES), BF16),
            pltpu.VMEM((coarse_slots, ROWS, LANES), BF16),
            pltpu.VMEM((coarse_slots, ROWS, LANES), BF16),
            pltpu.VMEM((slots, ROWS, LANES), F32),
            pltpu.VMEM((coarse_slots, ROWS, LANES), F32),
            pltpu.VMEM((members, ROWS, LANES), F32),
            pltpu.VMEM((coarse_slots, ROWS, LANES), F32),
            pltpu.VMEM((2, ROWS, STEP), F32),
            pltpu.VMEM((slots, rows, LANES), F32),
            pltpu.VMEM(m2l_table.shape, BF16),
            pltpu.VMEM(fine_pairs.shape, jnp.int32),
            pltpu.VMEM(coarse_pairs.shape, jnp.int32),
            pltpu.SMEM(fine_pairs.shape, jnp.int32),
            pltpu.SMEM(coarse_pairs.shape, jnp.int32),
            pltpu.SemaphoreType.DMA((5,)),
            pltpu.SemaphoreType.DMA((slots,)),
            pltpu.SemaphoreType.DMA((slots,)),
            pltpu.SemaphoreType.DMA((slots,)),
            pltpu.SemaphoreType.DMA((slots,)),
        ],
        compiler_params=pltpu.CompilerParams(
            vmem_limit_bytes=48 * 1024 * 1024, collective_id=0, has_side_effects=True
        ),
    )(mine, m2l_table, fine_pairs, coarse_pairs)


def solution(mesh):
    cells = P(None, ("runs", "space", "sub", "lane"))
    return jax.shard_map(
        functools.partial(per_device, mesh.shape["space"]),
        mesh=mesh,
        in_specs=(cells, cells, P(), cells, cells),
        out_specs=(cells, cells),
        check_vma=False,
    )
```

```python
import functools

import jax
import jax.numpy as jnp
from jax import lax
from jax.experimental import pallas as pl
from jax.experimental.pallas import tpu as pltpu
from jax.sharding import PartitionSpec as P

BLK = 128
STEP = 256
PUT = 512
LANES = 256
ROWS = 96
F32 = jnp.float32
BF16 = jnp.bfloat16


def divider(width, limit):
    for shift in range(31):
        mul = -(-(1 << shift) // width)
        if all((w * mul) >> shift == w // width for w in range(limit)):
            break
    assert limit * mul < 2**31
    return lambda w: (w * mul) >> shift


def row_sign(rows, dtype):
    index = lax.broadcasted_iota(jnp.int32, (rows, 1), 0)
    degree = jnp.zeros((rows, 1), jnp.int32)
    for root in range(1, 17):
        degree = degree + jnp.where(index >= root * root, 1, 0)
    return (1 - 2 * (degree & 1)).astype(F32).astype(dtype)


def split(values):
    top = values.astype(BF16)
    return top, (values - top.astype(F32)).astype(BF16)


def one_hot(lo):
    index = lax.broadcasted_iota(jnp.int32, (LANES, lo.shape[1]), 0)
    return jnp.where(index == lo, 1.0, 0.0).astype(BF16)


def pick(stack, hi, hot):
    count, height, _ = stack.shape
    block = stack[...].reshape(count * height, LANES)
    all_parts = jnp.dot(block, hot, preferred_element_type=F32)
    got = jnp.zeros((height, hi.shape[1]), F32)
    for h in range(count):
        got = jnp.where(hi == h, all_parts[h * height : (h + 1) * height], got)
    return got


def locate(cells, live, offset, width, first, limit):
    cells = cells - offset
    hi = divider(width, limit)(cells)
    return jnp.where(live, hi - first, -1), cells - hi * width


def translate(pairs, classes, table, stack, flipped, results, offset, width, first, limit):
    kinds = table.shape[0]
    k = table.shape[1]
    to_tgt, to_tgt_rest, to_src, to_src_rest = results

    def step(i, carry):
        base = pl.multiple_of(i * STEP, STEP)
        live = pairs[2:3, pl.ds(base, STEP)] < kinds
        src_hi, src_lo = locate(pairs[0:1, pl.ds(base, STEP)], live, offset, width, 0, limit)
        tgt_hi, tgt_lo = locate(pairs[1:2, pl.ds(base, STEP)], live, offset, width, first, limit)
        from_src = pick(stack, src_hi, one_hot(src_lo))
        from_tgt = pick(flipped, tgt_hi, one_hot(tgt_lo))
        for j in range(STEP // BLK):
            at = slice(j * BLK, (j + 1) * BLK)
            here = pl.ds(pl.multiple_of(base + j * BLK, BLK), BLK)
            operand = jnp.concatenate([from_src[:, at], from_tgt[:, at]], axis=1).astype(BF16)
            kind = jnp.minimum(classes[2, base + j * BLK], kinds - 1)
            moved = jnp.dot(table[kind], operand[:k], preferred_element_type=F32)
            top, rest = split(moved)
            to_tgt[:k, here] = top[:, :BLK]
            to_tgt_rest[:k, here] = rest[:, :BLK]
            to_src[:k, here] = top[:, BLK:]
            to_src_rest[:k, here] = rest[:, BLK:]
        return carry

    lax.fori_loop(0, pairs.shape[1] // STEP, step, 0, unroll=2)


def scatter(pairs, row, kinds, acc, starts, results, offset, width, limit):
    count, height, _ = acc.shape
    top, rest = results
    n = PUT

    def step(i, carry):
        at = pl.ds(pl.multiple_of(i * n, n), n)
        live = pairs[2:3, at] < kinds
        hi, lo = locate(pairs[row : row + 1, at], live, offset, width, 0, limit)
        hot = one_hot(lo)
        both = jnp.concatenate([top[:, at], rest[:, at]], axis=1)
        hi = jnp.concatenate([hi, hi], axis=1)
        spread = jnp.concatenate(
            [both * jnp.where(hi == h, 1.0, 0.0).astype(BF16) for h in starts], axis=0
        )
        total = lax.dot_general(
            spread,
            jnp.concatenate([hot, hot], axis=1),
            (((1,), (1,)), ((), ())),
            preferred_element_type=F32,
        )
        acc[...] += total.reshape(count, height, LANES)
        return carry

    lax.fori_loop(0, pairs.shape[1] // n, step, 0)


def kernel(
    sizes,
    fine_moments,
    coarse_moments,
    table_hbm,
    fine_hbm,
    coarse_hbm,
    fine_out,
    coarse_out,
    mine,
    window,
    fine_flip,
    coarse_stack,
    coarse_flip,
    away,
    home,
    coarse_src,
    coarse_tgt,
    fine_tgt,
    total,
    fine_results,
    coarse_results,
    arrived,
    table,
    fine_pairs,
    coarse_pairs,
    fine_classes,
    coarse_classes,
    local_sems,
    send_in,
    recv_in,
    send_out,
    recv_out,
):
    cf, cc, subs, lanes, spaces = sizes
    members = subs * lanes
    k = fine_out.shape[0]
    rows = arrived.shape[1]
    space = lax.axis_index("space")
    me = lax.axis_index("sub") * lanes + lax.axis_index("lane")

    local = [
        pltpu.make_async_copy(source, target, local_sems.at[n])
        for n, (source, target) in enumerate(
            (
                (table_hbm, table),
                (fine_hbm, fine_pairs),
                (coarse_hbm, coarse_pairs),
                (fine_hbm, fine_classes),
                (coarse_hbm, coarse_classes),
            )
        )
    ]
    for copy in local:
        copy.start()

    def partners(act, steps=(-1, 1, 0)):
        for step in steps:
            for member in range(members):
                there = space + step
                near = jnp.logical_and(there >= 0, there < spaces)
                if step == 0:
                    near = member != me
                target = {
                    "space": there,
                    "sub": jnp.int32(member // lanes),
                    "lane": jnp.int32(member % lanes),
                }
                theirs = (1 + step) * members + member
                ours = (1 - step) * members + me
                pl.when(near)(functools.partial(act, target, theirs, ours))

    barrier = pltpu.get_barrier_semaphore()

    def greet(target, theirs, ours):
        pl.semaphore_signal(
            barrier, inc=1, device_id=target, device_id_type=pl.DeviceIdType.MESH
        )

    partners(greet)
    mine[...] = jnp.zeros(mine.shape, BF16)
    mine[:k, :cf] = fine_moments[...]
    mine[:k, cf : cf + cc] = coarse_moments[...].astype(F32).T.astype(BF16)
    window[pl.ds(members + me, 1)] = mine[...][None]
    for step in (-1, 1):
        there = space + step
        first = (1 + step) * members

        @pl.when(jnp.logical_not(jnp.logical_and(there >= 0, there < spaces)))
        def _():
            window[first : first + members] = jnp.zeros((members, ROWS, LANES), BF16)

    beside = jnp.where(space > 0, 1, 0) + jnp.where(space < spaces - 1, 1, 0)
    pl.semaphore_wait(barrier, members - 1 + members * beside)

    def give(target, theirs, ours):
        return pltpu.make_async_remote_copy(
            src_ref=mine,
            dst_ref=window.at[ours],
            send_sem=send_in.at[theirs],
            recv_sem=recv_in.at[ours],
            device_id=target,
            device_id_type=pl.DeviceIdType.MESH,
        )

    def take(target, theirs, ours):
        return pltpu.make_async_remote_copy(
            src_ref=mine,
            dst_ref=window.at[theirs],
            send_sem=send_in.at[theirs],
            recv_sem=recv_in.at[theirs],
            device_id=target,
            device_id_type=pl.DeviceIdType.MESH,
        )

    partners(lambda *at: give(*at).start())
    for ref in (away, home, coarse_src, coarse_tgt, fine_tgt):
        ref[...] = jnp.zeros(ref.shape, ref.dtype)
    coarse_stack[...] = jnp.zeros(coarse_stack.shape, BF16)
    partners(lambda *at: take(*at).wait_recv())
    partners(lambda *at: give(*at).wait_send())

    sign_b = row_sign(ROWS, BF16)
    sign_f = row_sign(ROWS, F32)
    fine_flip[...] = window[members : 2 * members] * sign_b
    for slot in range(3 * members):
        h, at = divmod(slot * cc, LANES)
        coarse_stack[h, :, at : at + cc] = window[slot, :, cf : cf + cc]
    coarse_flip[...] = coarse_stack[...] * sign_b
    for copy in local:
        copy.wait()
    kinds = table.shape[0]
    fine_at = ((space - 1) * members * cf, cf)
    coarse_at = ((space - 1) * members * cc, LANES)
    fine_limit, coarse_limit = 3 * members * cf, 3 * members * cc
    fine_parts = [fine_results.at[n] for n in range(4)]
    coarse_parts = [coarse_results.at[n] for n in range(4)]
    translate(
        coarse_pairs, coarse_classes, table, coarse_stack, coarse_flip, coarse_parts,
        *coarse_at, 0, coarse_limit,
    )
    translate(
        fine_pairs, fine_classes, table, window, fine_flip, fine_parts,
        *fine_at, members, fine_limit,
    )
    coarse_slots = range(coarse_src.shape[0])
    scatter(
        coarse_pairs, 0, kinds, coarse_src, coarse_slots, coarse_parts[2:], *coarse_at,
        coarse_limit,
    )
    scatter(
        coarse_pairs, 1, kinds, coarse_tgt, coarse_slots, coarse_parts[:2], *coarse_at,
        coarse_limit,
    )
    coarse_src[...] = coarse_src[...] * sign_f + coarse_tgt[...]

    def finish(ref, at, slot, more=None):
        value = ref[at] * sign_f
        ref[at] = value if more is None else value + more
        h, lane = divmod(slot * cc, LANES)
        ref[at, :, cf : cf + cc] = coarse_src[h, :, lane : lane + cc]

    inside = list(range(members, 2 * members))
    outside = [slot for slot in range(3 * members) if slot not in inside]
    scatter(
        fine_pairs, 0, kinds, away, outside, fine_parts[2:], *fine_at, fine_limit
    )
    for at, slot in enumerate(outside):
        finish(away, at, slot)

    def source(theirs):
        if theirs in inside:
            return home.at[theirs - members, 0:rows]
        return away.at[outside.index(theirs), 0:rows]

    def hand(target, theirs, ours):
        return pltpu.make_async_remote_copy(
            src_ref=source(theirs),
            dst_ref=arrived.at[ours],
            send_sem=send_out.at[theirs],
            recv_sem=recv_out.at[ours],
            device_id=target,
            device_id_type=pl.DeviceIdType.MESH,
        )

    def catch(target, theirs, ours):
        return pltpu.make_async_remote_copy(
            src_ref=source(theirs),
            dst_ref=arrived.at[theirs],
            send_sem=send_out.at[theirs],
            recv_sem=recv_out.at[theirs],
            device_id=target,
            device_id_type=pl.DeviceIdType.MESH,
        )

    def gather(target, theirs, ours):
        catch(target, theirs, ours).wait_recv()
        total[...] += arrived[theirs]

    partners(lambda *at: hand(*at).start(), (-1, 1))
    scatter(
        fine_pairs, 0, kinds, home, inside, fine_parts[2:], *fine_at, fine_limit
    )
    scatter(
        fine_pairs, 1, kinds, fine_tgt, inside, fine_parts[:2], *fine_at, fine_limit
    )
    for at, slot in enumerate(inside):
        finish(home, at, slot, fine_tgt[at])
    partners(lambda *at: hand(*at).start(), (0,))
    total[...] = home[pl.ds(me, 1), 0:rows][0]
    partners(gather, (-1, 1))
    partners(gather, (0,))
    fine_out[...] = total[:k, :cf]
    coarse_out[...] = total[:, cf : cf + cc].T[:, :k]
    partners(lambda *at: hand(*at).wait_send())


def per_device(spaces, fine_moments, coarse_moments, m2l_table, fine_pairs, coarse_pairs):
    k, cf = fine_moments.shape
    cc = coarse_moments.shape[1]
    subs, lanes = lax.axis_size("sub"), lax.axis_size("lane")
    members = subs * lanes
    slots = 3 * members
    rows = -(-k // 8) * 8
    coarse_slots = -(-slots * cc // LANES)
    vmem = pl.BlockSpec(memory_space=pltpu.VMEM)
    anywhere = pl.BlockSpec(memory_space=pl.ANY)
    fine_local, coarse_local = pl.pallas_call(
        functools.partial(kernel, (cf, cc, subs, lanes, spaces)),
        out_shape=(
            jax.ShapeDtypeStruct((k, cf), F32),
            jax.ShapeDtypeStruct((cc, k), F32),
        ),
        in_specs=[vmem, vmem, anywhere, anywhere, anywhere],
        out_specs=(vmem, vmem),
        scratch_shapes=[
            pltpu.VMEM((ROWS, LANES), BF16),
            pltpu.VMEM((slots, ROWS, LANES), BF16),
            pltpu.VMEM((members, ROWS, LANES), BF16),
            pltpu.VMEM((coarse_slots, ROWS, LANES), BF16),
            pltpu.VMEM((coarse_slots, ROWS, LANES), BF16),
            pltpu.VMEM((2 * members, ROWS, LANES), F32),
            pltpu.VMEM((members, ROWS, LANES), F32),
            pltpu.VMEM((coarse_slots, ROWS, LANES), F32),
            pltpu.VMEM((coarse_slots, ROWS, LANES), F32),
            pltpu.VMEM((members, ROWS, LANES), F32),
            pltpu.VMEM((rows, LANES), F32),
            pltpu.VMEM((4, ROWS, fine_pairs.shape[1]), BF16),
            pltpu.VMEM((4, ROWS, coarse_pairs.shape[1]), BF16),
            pltpu.VMEM((slots, rows, LANES), F32),
            pltpu.VMEM(m2l_table.shape, BF16),
            pltpu.VMEM(fine_pairs.shape, jnp.int32),
            pltpu.VMEM(coarse_pairs.shape, jnp.int32),
            pltpu.SMEM(fine_pairs.shape, jnp.int32),
            pltpu.SMEM(coarse_pairs.shape, jnp.int32),
            pltpu.SemaphoreType.DMA((5,)),
            pltpu.SemaphoreType.DMA((slots,)),
            pltpu.SemaphoreType.DMA((slots,)),
            pltpu.SemaphoreType.DMA((slots,)),
            pltpu.SemaphoreType.DMA((slots,)),
        ],
        compiler_params=pltpu.CompilerParams(
            vmem_limit_bytes=48 * 1024 * 1024, collective_id=0, has_side_effects=True
        ),
    )(fine_moments, coarse_moments.T, m2l_table, fine_pairs, coarse_pairs)
    return fine_local, coarse_local.T


def solution(mesh):
    cells = P(None, ("runs", "space", "sub", "lane"))
    return jax.shard_map(
        functools.partial(per_device, mesh.shape["space"]),
        mesh=mesh,
        in_specs=(cells, cells, P(), cells, cells),
        out_specs=(cells, cells),
        check_vma=False,
    )
```

```python
import functools

import jax
import jax.numpy as jnp
from jax import lax
from jax.experimental import pallas as pl
from jax.experimental.pallas import tpu as pltpu
from jax.sharding import PartitionSpec as P

BLK = 128
STEP = 512
PUT = 1024
UNROLL = 2
LANES = 256
ROWS = 96
F32 = jnp.float32
BF16 = jnp.bfloat16


def divider(width, limit):
    for shift in range(31):
        mul = -(-(1 << shift) // width)
        if all((w * mul) >> shift == w // width for w in range(limit)):
            break
    assert limit * mul < 2**31
    return lambda w: (w * mul) >> shift


def row_sign(rows, dtype):
    index = lax.broadcasted_iota(jnp.int32, (rows, 1), 0)
    degree = jnp.zeros((rows, 1), jnp.int32)
    for root in range(1, 17):
        degree = degree + jnp.where(index >= root * root, 1, 0)
    return (1 - 2 * (degree & 1)).astype(F32).astype(dtype)


def split(values):
    top = values.astype(BF16)
    return top, (values - top.astype(F32)).astype(BF16)


def one_hot(lo):
    index = lax.broadcasted_iota(jnp.int32, (LANES, lo.shape[1]), 0)
    return jnp.where(index == lo, 1.0, 0.0).astype(BF16)


def pick(stack, hi, hot):
    count, height, _ = stack.shape
    block = stack[...].reshape(count * height, LANES)
    all_parts = jnp.dot(block, hot, preferred_element_type=F32)
    got = jnp.zeros((height, hi.shape[1]), F32)
    for h in range(count):
        got = jnp.where(hi == h, all_parts[h * height : (h + 1) * height], got)
    return got


def locate(cells, live, offset, width, first, limit):
    cells = cells - offset
    hi = divider(width, limit)(cells)
    return jnp.where(live, hi - first, -1), cells - hi * width


def fetch_targets(pairs, kinds, flipped, fetched, offset, width, first, limit):
    def step(i, carry):
        at = pl.ds(pl.multiple_of(i * STEP, STEP), STEP)
        live = pairs[2:3, at] < kinds
        hi, lo = locate(pairs[1:2, at], live, offset, width, first, limit)
        fetched[:, at] = pick(flipped, hi, one_hot(lo)).astype(BF16)
        return carry

    lax.fori_loop(0, pairs.shape[1] // STEP, step, 0, unroll=UNROLL)


def translate(pairs, classes, table, stack, fetched, results, offset, width, limit):
    kinds = table.shape[0]
    k = table.shape[1]
    to_tgt, to_tgt_rest, to_src, to_src_rest = results

    def step(i, carry):
        base = pl.multiple_of(i * STEP, STEP)
        live = pairs[2:3, pl.ds(base, STEP)] < kinds
        src_hi, src_lo = locate(pairs[0:1, pl.ds(base, STEP)], live, offset, width, 0, limit)
        from_src = pick(stack, src_hi, one_hot(src_lo)).astype(BF16)
        from_tgt = fetched[:, pl.ds(base, STEP)]
        for j in range(STEP // BLK):
            at = slice(j * BLK, (j + 1) * BLK)
            here = pl.ds(pl.multiple_of(base + j * BLK, BLK), BLK)
            operand = jnp.concatenate([from_src[:, at], from_tgt[:, at]], axis=1)
            kind = jnp.minimum(classes[2, base + j * BLK], kinds - 1)
            moved = jnp.dot(table[kind], operand[:k], preferred_element_type=F32)
            top, rest = split(moved)
            to_tgt[:k, here] = top[:, :BLK]
            to_tgt_rest[:k, here] = rest[:, :BLK]
            to_src[:k, here] = top[:, BLK:]
            to_src_rest[:k, here] = rest[:, BLK:]
        return carry

    lax.fori_loop(0, pairs.shape[1] // STEP, step, 0, unroll=UNROLL)


def scatter(pairs, row, kinds, acc, starts, results, offset, width, limit):
    count, height, _ = acc.shape
    top, rest = results
    n = PUT

    def step(i, carry):
        at = pl.ds(pl.multiple_of(i * n, n), n)
        live = pairs[2:3, at] < kinds
        hi, lo = locate(pairs[row : row + 1, at], live, offset, width, 0, limit)
        hot = one_hot(lo)
        both = jnp.concatenate([top[:, at], rest[:, at]], axis=1)
        hi = jnp.concatenate([hi, hi], axis=1)
        spread = jnp.concatenate(
            [both * jnp.where(hi == h, 1.0, 0.0).astype(BF16) for h in starts], axis=0
        )
        total = lax.dot_general(
            spread,
            jnp.concatenate([hot, hot], axis=1),
            (((1,), (1,)), ((), ())),
            preferred_element_type=F32,
        )
        acc[...] += total.reshape(count, height, LANES)
        return carry

    lax.fori_loop(0, pairs.shape[1] // n, step, 0)


def kernel(
    sizes,
    fine_moments,
    coarse_moments,
    table_hbm,
    fine_hbm,
    coarse_hbm,
    fine_out,
    coarse_out,
    mine,
    window,
    fine_flip,
    coarse_stack,
    coarse_flip,
    away,
    home,
    coarse_src,
    coarse_tgt,
    fine_tgt,
    total,
    fine_fetched,
    coarse_fetched,
    fine_results,
    coarse_results,
    arrived,
    table,
    fine_pairs,
    coarse_pairs,
    fine_classes,
    coarse_classes,
    local_sems,
    send_in,
    recv_in,
    send_out,
    recv_out,
):
    cf, cc, subs, lanes, spaces = sizes
    members = subs * lanes
    k = fine_out.shape[0]
    rows = arrived.shape[1]
    space = lax.axis_index("space")
    me = lax.axis_index("sub") * lanes + lax.axis_index("lane")

    local = [
        pltpu.make_async_copy(source, target, local_sems.at[n])
        for n, (source, target) in enumerate(
            (
                (table_hbm, table),
                (fine_hbm, fine_pairs),
                (coarse_hbm, coarse_pairs),
                (fine_hbm, fine_classes),
                (coarse_hbm, coarse_classes),
            )
        )
    ]
    for copy in local:
        copy.start()

    def partners(act, steps=(-1, 1, 0)):
        for step in steps:
            for member in range(members):
                there = space + step
                near = jnp.logical_and(there >= 0, there < spaces)
                if step == 0:
                    near = member != me
                target = {
                    "space": there,
                    "sub": jnp.int32(member // lanes),
                    "lane": jnp.int32(member % lanes),
                }
                theirs = (1 + step) * members + member
                ours = (1 - step) * members + me
                pl.when(near)(functools.partial(act, target, theirs, ours))

    barrier = pltpu.get_barrier_semaphore()

    def greet(target, theirs, ours):
        pl.semaphore_signal(
            barrier, inc=1, device_id=target, device_id_type=pl.DeviceIdType.MESH
        )

    partners(greet)
    mine[...] = jnp.zeros(mine.shape, BF16)
    mine[:k, :cf] = fine_moments[...]
    mine[:k, cf : cf + cc] = coarse_moments[...].astype(F32).T.astype(BF16)
    window[pl.ds(members + me, 1)] = mine[...][None]
    for step in (-1, 1):
        there = space + step
        first = (1 + step) * members

        @pl.when(jnp.logical_not(jnp.logical_and(there >= 0, there < spaces)))
        def _():
            window[first : first + members] = jnp.zeros((members, ROWS, LANES), BF16)

    beside = jnp.where(space > 0, 1, 0) + jnp.where(space < spaces - 1, 1, 0)
    pl.semaphore_wait(barrier, members - 1 + members * beside)

    def give(target, theirs, ours):
        return pltpu.make_async_remote_copy(
            src_ref=mine,
            dst_ref=window.at[ours],
            send_sem=send_in.at[theirs],
            recv_sem=recv_in.at[ours],
            device_id=target,
            device_id_type=pl.DeviceIdType.MESH,
        )

    def take(target, theirs, ours):
        return pltpu.make_async_remote_copy(
            src_ref=mine,
            dst_ref=window.at[theirs],
            send_sem=send_in.at[theirs],
            recv_sem=recv_in.at[theirs],
            device_id=target,
            device_id_type=pl.DeviceIdType.MESH,
        )

    partners(lambda *at: give(*at).start(), (0, -1, 1))
    for ref in (away, home, coarse_src, coarse_tgt, fine_tgt):
        ref[...] = jnp.zeros(ref.shape, ref.dtype)
    coarse_stack[...] = jnp.zeros(coarse_stack.shape, BF16)
    sign_b = row_sign(ROWS, BF16)
    sign_f = row_sign(ROWS, F32)
    kinds = table.shape[0]
    fine_at = ((space - 1) * members * cf, cf)
    coarse_at = ((space - 1) * members * cc, LANES)
    fine_limit, coarse_limit = 3 * members * cf, 3 * members * cc
    partners(lambda *at: take(*at).wait_recv(), (0,))
    fine_flip[...] = window[members : 2 * members] * sign_b
    for copy in local:
        copy.wait()
    fetch_targets(
        fine_pairs, kinds, fine_flip, fine_fetched, *fine_at, members, fine_limit
    )
    partners(lambda *at: take(*at).wait_recv(), (-1, 1))
    partners(lambda *at: give(*at).wait_send())
    for slot in range(3 * members):
        h, at = divmod(slot * cc, LANES)
        coarse_stack[h, :, at : at + cc] = window[slot, :, cf : cf + cc]
    coarse_flip[...] = coarse_stack[...] * sign_b
    fetch_targets(
        coarse_pairs, kinds, coarse_flip, coarse_fetched, *coarse_at, 0, coarse_limit
    )
    fine_parts = [fine_results.at[n] for n in range(4)]
    coarse_parts = [coarse_results.at[n] for n in range(4)]
    translate(
        coarse_pairs, coarse_classes, table, coarse_stack, coarse_fetched, coarse_parts,
        *coarse_at, coarse_limit,
    )
    translate(
        fine_pairs, fine_classes, table, window, fine_fetched, fine_parts,
        *fine_at, fine_limit,
    )
    coarse_slots = range(coarse_src.shape[0])
    scatter(
        coarse_pairs, 0, kinds, coarse_src, coarse_slots, coarse_parts[2:], *coarse_at,
        coarse_limit,
    )
    scatter(
        coarse_pairs, 1, kinds, coarse_tgt, coarse_slots, coarse_parts[:2], *coarse_at,
        coarse_limit,
    )
    coarse_src[...] = coarse_src[...] * sign_f + coarse_tgt[...]

    def finish(ref, at, slot, more=None):
        value = ref[at] * sign_f
        ref[at] = value if more is None else value + more
        h, lane = divmod(slot * cc, LANES)
        ref[at, :, cf : cf + cc] = coarse_src[h, :, lane : lane + cc]

    inside = list(range(members, 2 * members))
    outside = [slot for slot in range(3 * members) if slot not in inside]
    scatter(
        fine_pairs, 0, kinds, away, outside, fine_parts[2:], *fine_at, fine_limit
    )
    for at, slot in enumerate(outside):
        finish(away, at, slot)

    def source(theirs):
        if theirs in inside:
            return home.at[theirs - members, 0:rows]
        return away.at[outside.index(theirs), 0:rows]

    def hand(target, theirs, ours):
        return pltpu.make_async_remote_copy(
            src_ref=source(theirs),
            dst_ref=arrived.at[ours],
            send_sem=send_out.at[theirs],
            recv_sem=recv_out.at[ours],
            device_id=target,
            device_id_type=pl.DeviceIdType.MESH,
        )

    def catch(target, theirs, ours):
        return pltpu.make_async_remote_copy(
            src_ref=source(theirs),
            dst_ref=arrived.at[theirs],
            send_sem=send_out.at[theirs],
            recv_sem=recv_out.at[theirs],
            device_id=target,
            device_id_type=pl.DeviceIdType.MESH,
        )

    def gather(target, theirs, ours):
        catch(target, theirs, ours).wait_recv()
        total[...] += arrived[theirs]

    partners(lambda *at: hand(*at).start(), (-1, 1))
    scatter(
        fine_pairs, 0, kinds, home, inside, fine_parts[2:], *fine_at, fine_limit
    )
    scatter(
        fine_pairs, 1, kinds, fine_tgt, inside, fine_parts[:2], *fine_at, fine_limit
    )
    for at, slot in enumerate(inside):
        finish(home, at, slot, fine_tgt[at])
    partners(lambda *at: hand(*at).start(), (0,))
    total[...] = home[pl.ds(me, 1), 0:rows][0]
    partners(gather, (-1, 1))
    partners(gather, (0,))
    fine_out[...] = total[:k, :cf]
    coarse_out[...] = total[:, cf : cf + cc].T[:, :k]
    partners(lambda *at: hand(*at).wait_send())


def per_device(spaces, fine_moments, coarse_moments, m2l_table, fine_pairs, coarse_pairs):
    k, cf = fine_moments.shape
    cc = coarse_moments.shape[1]
    subs, lanes = lax.axis_size("sub"), lax.axis_size("lane")
    members = subs * lanes
    slots = 3 * members
    rows = -(-k // 8) * 8
    coarse_slots = -(-slots * cc // LANES)
    vmem = pl.BlockSpec(memory_space=pltpu.VMEM)
    anywhere = pl.BlockSpec(memory_space=pl.ANY)
    fine_local, coarse_local = pl.pallas_call(
        functools.partial(kernel, (cf, cc, subs, lanes, spaces)),
        out_shape=(
            jax.ShapeDtypeStruct((k, cf), F32),
            jax.ShapeDtypeStruct((cc, k), F32),
        ),
        in_specs=[vmem, vmem, anywhere, anywhere, anywhere],
        out_specs=(vmem, vmem),
        scratch_shapes=[
            pltpu.VMEM((ROWS, LANES), BF16),
            pltpu.VMEM((slots, ROWS, LANES), BF16),
            pltpu.VMEM((members, ROWS, LANES), BF16),
            pltpu.VMEM((coarse_slots, ROWS, LANES), BF16),
            pltpu.VMEM((coarse_slots, ROWS, LANES), BF16),
            pltpu.VMEM((2 * members, ROWS, LANES), F32),
            pltpu.VMEM((members, ROWS, LANES), F32),
            pltpu.VMEM((coarse_slots, ROWS, LANES), F32),
            pltpu.VMEM((coarse_slots, ROWS, LANES), F32),
            pltpu.VMEM((members, ROWS, LANES), F32),
            pltpu.VMEM((rows, LANES), F32),
            pltpu.VMEM((ROWS, fine_pairs.shape[1]), BF16),
            pltpu.VMEM((ROWS, coarse_pairs.shape[1]), BF16),
            pltpu.VMEM((4, ROWS, fine_pairs.shape[1]), BF16),
            pltpu.VMEM((4, ROWS, coarse_pairs.shape[1]), BF16),
            pltpu.VMEM((slots, rows, LANES), F32),
            pltpu.VMEM(m2l_table.shape, BF16),
            pltpu.VMEM(fine_pairs.shape, jnp.int32),
            pltpu.VMEM(coarse_pairs.shape, jnp.int32),
            pltpu.SMEM(fine_pairs.shape, jnp.int32),
            pltpu.SMEM(coarse_pairs.shape, jnp.int32),
            pltpu.SemaphoreType.DMA((5,)),
            pltpu.SemaphoreType.DMA((slots,)),
            pltpu.SemaphoreType.DMA((slots,)),
            pltpu.SemaphoreType.DMA((slots,)),
            pltpu.SemaphoreType.DMA((slots,)),
        ],
        compiler_params=pltpu.CompilerParams(
            vmem_limit_bytes=48 * 1024 * 1024, collective_id=0, has_side_effects=True
        ),
    )(fine_moments, coarse_moments.T, m2l_table, fine_pairs, coarse_pairs)
    return fine_local, coarse_local.T


def solution(mesh):
    cells = P(None, ("runs", "space", "sub", "lane"))
    return jax.shard_map(
        functools.partial(per_device, mesh.shape["space"]),
        mesh=mesh,
        in_specs=(cells, cells, P(), cells, cells),
        out_specs=(cells, cells),
        check_vma=False,
    )
```
